256 devices in a mesh: mp: 2 (over x_hi), tp: 16 (over z, core), dp: 8 (over y, x_lo).
Axes of the slice: x: 4 (x_hi: 2, x_lo: 2; x = x_hi * 2 + x_lo), y: 4, z: 8, core: 2. Of those that a mesh axis runs over, the one named last changes fastest.
Arguments:
- hidden: bfloat16 [2, 1024, 28672], P('mp', 'dp', 'tp'), may hold values from -8 to 8
- down_weight: bfloat16 [2, 28672, 8192], P('mp', 'tp', 'dp'), may hold values from -0.03125 to 0.03125
- whitening: bfloat16 [2, 8192, 8192], P('mp', 'dp', 'tp'), may hold values from -0.0625 to 0.0625
Outputs:
- cross: float32 [8192, 8192], P(('mp', 'dp'), 'tp')
The draws below stay inside these ranges and needn't reach their ends.
All inputs are finite; a program needn't handle non-finite values.
Results may differ from the reference program's by a relative error of at most 0.0093.
Values may be sent and summed in bfloat16 or wider, within the bound.
A program may use at most 64 MiB of HBM per device.

```python
import math
import jax
import jax.numpy as jnp
from jax import lax

D = 8192
FF = 28672
TOKENS = 1024


def draw_hidden(key, part):
    key = jax.random.fold_in(key, 11)
    offset_key, noise_key = jax.random.split(key)
    noise = jax.random.normal(noise_key, (2, TOKENS, FF), jnp.float32)
    offsets = 0.8 * jax.random.normal(offset_key, (2, 1, FF), jnp.float32)
    return jnp.clip(noise + offsets, -8.0, 8.0).astype(jnp.bfloat16)


def level_of(stream_key, shape, cuts, smallest, largest):
    factor_of, own = 1.0, jax.random.fold_in(stream_key, 6)
    for axis_at, shards_of in cuts:
        steps = jnp.exp(jax.random.uniform(jax.random.fold_in(own, axis_at), (shards_of,), jnp.float32, smallest / len(cuts), largest / len(cuts)))
        factor_of = factor_of * jnp.repeat(steps, shape[axis_at] // shards_of).reshape([-1 if axis == axis_at else 1 for axis in range(len(shape))])
    return factor_of


def centred(rng, dims, width, reach, cuts=(), dtype=jnp.bfloat16):
    values = width * jax.random.normal(rng, dims, jnp.float32)
    if cuts:
        values = values * level_of(rng, dims, cuts, -0.22, 0.18)
    return jnp.clip(values, -reach, reach).astype(dtype)


def setup_inputs(seed: int = 0) -> dict:
    key_list = jax.random.split(jax.random.key(seed), 4)
    return {
        "hidden": draw_hidden(jax.random.fold_in(key_list[3], 71), 0),
        "down_weight": centred(key_list[1], (2, FF, D), FF ** -0.5, 0.03125, ((0, 2), (1, 16), (2, 8))),
        "whitening": centred(key_list[2], (2, D, D), D ** -0.5, 0.0625, ((0, 2), (1, 8), (2, 16))),
    }


def reference(hidden, down_weight, whitening):
    whites = []
    for model in range(2):
        outputs = jnp.dot(hidden[model], down_weight[model], preferred_element_type=jnp.float32).astype(jnp.bfloat16)
        wide = outputs.astype(jnp.float32)
        mean = lax.optimization_barrier(jnp.mean(wide, axis=0, keepdims=True))
        centered = (wide - mean).astype(jnp.bfloat16)
        white = jnp.dot(centered, whitening[model], preferred_element_type=jnp.float32).astype(jnp.bfloat16)
        whites.append(white)
    cross = lax.dot_general(whites[0], whites[1], (((0,), (0,)), ((), ())), preferred_element_type=jnp.float32)
    return cross * (1.0 / math.sqrt(TOKENS))
```

```python
import math

import jax
import jax.numpy as jnp
from jax import lax
from jax.experimental import pallas as pl
from jax.experimental.pallas import tpu as pltpu
from jax.sharding import PartitionSpec as P

MESH = pl.DeviceIdType.MESH
F32, BF16 = jnp.float32, jnp.bfloat16
TILE = 256
SHIFTS = (0, -1, 1, 2)
PENDING = ((), (12,), (13,), (3, 8, 4, 9))
ORDER = (
    "near", 0, 0, "far", 1, 1, 0, 2, 0, 2, 0, 1, 0, 0, 1, 2, 1, 0, 3, 3, 1, 2, 1, 2, 1, 3, 2, 2, 3, 2, 3, 3, 3, 3,
)


def kernel(
    hid, wgt, fac, out,
    acts, weights, factor, sums, own, give, take, parts, reduced, outs,
    wpart, wown, wland, white, qwen, llama,
    load_sem, near_sem, sum_sem, pair_sem, ring_sem, all_sem, core_sem, dp_sem, mp_sem, row_sem, spread_sem, last_sem,
):
    mp, tp, dp = lax.axis_index("mp"), lax.axis_index("tp"), lax.axis_index("dp")
    z, core = tp // 2, tp % 2
    y, xlo = dp // 2, dp % 2
    tokens = hid.shape[1]
    half = tokens // 2
    group_rows = 2 * tokens
    piece = group_rows // 8
    width = wgt.shape[2]
    side = width // 2
    cols = fac.shape[2]

    def at(**coords):
        return {"mp": coords.get("mp", mp), "tp": coords.get("tp", tp), "dp": coords.get("dp", dp)}

    def rem(value, count):
        return lax.rem(value + count, count)

    started = []

    def copy(src, dst, sem, index, target, there=None):
        return pltpu.make_async_remote_copy(
            src_ref=src, dst_ref=dst, send_sem=sem.at[(0, *index)], recv_sem=sem.at[(1, *(there or index))],
            device_id=target, device_id_type=MESH,
        )

    def send(*args, **kw):
        c = copy(*args, **kw)
        c.start()
        started.append(c)

    def arrived(dst, sem, index):
        copy(dst, dst, sem, index, at()).wait_recv()

    row0 = pl.multiple_of(dp * tokens, tokens)
    loads = [
        pltpu.make_async_copy(hid.at[0], acts.at[pl.ds(row0, tokens)], load_sem.at[0]),
        pltpu.make_async_copy(wgt.at[0], weights, load_sem.at[1]),
        pltpu.make_async_copy(fac.at[0], factor, load_sem.at[2]),
    ]
    for load in loads:
        load.start()

    barrier = pltpu.get_barrier_semaphore()
    row_source = mp * 8 + dp
    greet = [at(dp=rem(dp + o, 8)) for o in range(1, 8)]
    greet += [at(tp=rem(tp + 2 * o, 16)) for o in range(1, 8)]
    greet += [at(tp=tp + 1 - 2 * core)]
    greet += [at(mp=1 - mp, dp=rem(dp + o, 8)) for o in range(8)]
    for target in greet:
        pl.semaphore_signal(barrier, inc=1, device_id=target, device_id_type=MESH)
    alone = (mp == 0) & (dp == 0) & (tp == 0)

    @pl.when(jnp.logical_not(alone))
    def _():
        pl.semaphore_signal(
            barrier, inc=1, device_id=at(mp=0, dp=z, tp=row_source), device_id_type=MESH
        )

    loads[0].wait()
    sums[dp] = jnp.sum(acts[pl.ds(row0, tokens), :].astype(F32), axis=0, keepdims=True)

    extra = jnp.where(mp == 0, jnp.where(alone, 1, 2), 0)
    pl.semaphore_wait(barrier, len(greet) + extra)

    for o in range(1, 8):
        send(sums.at[dp], sums.at[dp], sum_sem, (o,), at(dp=rem(dp + o, 8)))

    up, down, across = at(dp=rem(dp + 2, 8)), at(dp=rem(dp - 2, 8)), at(dp=dp + 1 - 2 * xlo)

    def rows(dy, other, which):
        x = 1 - xlo if other else xlo
        start = (rem(y + dy + 4, 4) * 2 + x) * tokens + which * half
        return acts.at[pl.ds(pl.multiple_of(start, half), half)]

    hops = {
        0: (up, 0, 0, 0), 1: (up, 0, 0, 1), 2: (up, 0, 1, 0), 3: (up, -1, 0, 0), 4: (up, -1, 1, 0),
        5: (down, 0, 0, 1), 6: (down, 0, 0, 0), 7: (down, 0, 1, 1), 8: (down, 1, 0, 1), 9: (down, 1, 1, 1),
        10: (across, 0, 0, 0), 11: (across, 0, 0, 1), 12: (across, -1, 0, 1), 13: (across, 1, 0, 0),
    }

    def hop(index):
        target, dy, other, which = hops[index]
        block = rows(dy, other, which)
        send(block, block, near_sem, (index,), target)

    def landed(index):
        target, dy, other, which = hops[index]
        if target is up:
            block = rows(dy - 1, other, which)
        elif target is down:
            block = rows(dy + 1, other, which)
        else:
            block = rows(dy, 1 - other, which)
        arrived(block, near_sem, (index,))

    for index in (10, 0, 5, 11, 1, 6):
        hop(index)

    loads[1].wait()
    for o in range(1, 8):
        arrived(sums.at[rem(dp - o, 8)], sum_sem, (o,))
    mean = jnp.sum(sums[...], axis=0) * (1.0 / 1024)
    high = mean.astype(BF16).astype(F32)
    line = lax.broadcasted_iota(jnp.int32, (16, mean.shape[1]), 0)
    pair = jnp.where(line == 0, high, jnp.where(line == 1, mean - high, 0.0)).astype(BF16)
    shift = jnp.sum(jnp.dot(pair, weights[...], preferred_element_type=F32), axis=0, keepdims=True)
    own_shift = jnp.where(core == 0, shift[:, :side], shift[:, side:])
    other_shift = jnp.where(core == 0, shift[:, side:], shift[:, :side])

    sibling = at(tp=tp + 1 - 2 * core)
    sign = 1 - 2 * core
    ahead, behind = at(tp=rem(tp + 2 * sign, 16)), at(tp=rem(tp - 2 * sign, 16))

    def group(g):
        base = rem(y + SHIFTS[g], 4) * group_rows
        base = pl.multiple_of(base, group_rows)
        block = acts.at[pl.ds(base, group_rows)]

        def partial(dst, first, offset):
            for n in range(side // TILE):
                columns = pl.ds(pl.multiple_of(first + n * TILE, TILE), TILE)
                here = pl.ds(n * TILE, TILE)
                dst[g, :, here] = (
                    jnp.dot(block[...], weights[:, columns], preferred_element_type=F32)
                    - offset[:, n * TILE:(n + 1) * TILE]
                )

        for index in PENDING[g]:
            landed(index)
        partial(give, (1 - core) * side, other_shift)
        send(give.at[g], take.at[g], pair_sem, (g,), sibling)
        partial(own, core * side, own_shift)
        yield
        arrived(take.at[g], pair_sem, (g,))
        total = own[g] + take[g]
        own[g] = total
        parts[g] = total.astype(BF16)
        for o in (4, 3, 5, 2, 6, 1, 7):
            to = rem(z + o, 8)
            send(
                parts.at[g, pl.ds(pl.multiple_of(to * piece, piece), piece)], reduced.at[g, o],
                ring_sem, (g, o), at(tp=rem(tp + 2 * o, 16)),
            )
        yield
        here = pl.ds(pl.multiple_of(z * piece, piece), piece)
        result = own[g, here, :]
        for o in (1, 7, 2, 6, 3, 5, 4):
            arrived(reduced.at[g, o], ring_sem, (g, o))
            result = result + reduced[g, o].astype(F32)
        mine = pl.ds(pl.multiple_of(core * side, side), side)

        def chunk(distance):
            start = base + rem(z + distance + 8, 8) * piece
            return outs.at[pl.ds(pl.multiple_of(start, piece), piece), mine]

        outs[pl.ds(pl.multiple_of(base + z * piece, piece), piece), mine] = result.astype(BF16)
        send(chunk(0), chunk(0), all_sem, (g, 1), ahead)
        send(chunk(0), chunk(0), all_sem, (g, 5), behind)
        for step in (1, 2, 3):
            yield
            block_a = chunk(-sign * step)
            arrived(block_a, all_sem, (g, step))
            send(block_a, block_a, all_sem, (g, step + 1), ahead)
            block_b = chunk(sign * step)
            arrived(block_b, all_sem, (g, 4 + step))
            if step < 3:
                send(block_b, block_b, all_sem, (g, 5 + step), behind)
        yield
        arrived(chunk(-sign * 4), all_sem, (g, 4))
        whole = outs.at[pl.ds(base, group_rows), mine]
        send(whole, whole, core_sem, (g,), sibling)
        yield
        theirs = pl.ds(pl.multiple_of((1 - core) * side, side), side)
        arrived(outs.at[pl.ds(base, group_rows), theirs], core_sem, (g,))
        if g == 0:
            loads[2].wait()
        for n in range(cols // TILE):
            here = pl.ds(n * TILE, TILE)
            product = jnp.dot(
                outs[pl.ds(base, group_rows), :], factor[:, here], preferred_element_type=F32
            )
            if g == 0:
                mine_first = xlo == 0
                wown[:, here] = jnp.where(mine_first, product[:tokens], product[tokens:])
            wpart[g, :, here] = product.astype(BF16)
        owner = rem(y + SHIFTS[g] + 4, 4) * 2
        for cross in (0, 1):
            if g == 0 and cross == 0:
                continue
            x = 1 - xlo if cross else xlo
            send(
                wpart.at[g, pl.ds(pl.multiple_of(x * tokens, tokens), tokens)], wland.at[g, cross],
                dp_sem, (g, cross), at(dp=owner + x),
            )
        yield

    groups = [group(g) for g in range(4)]
    for name in ORDER:
        if name == "near":
            for incoming, outgoing in ((10, 2), (0, 3), (5, 8), (11, 7), (1, 12), (6, 13)):
                landed(incoming)
                hop(outgoing)
        elif name == "far":
            for incoming, outgoing in ((2, 4), (7, 9)):
                landed(incoming)
                hop(outgoing)
        else:
            next(groups[name])

    result = wown[...]
    for g in range(4):
        for cross in (0, 1):
            if g or cross:
                arrived(wland.at[g, cross], dp_sem, (g, cross))
                result = result + wland[g, cross].astype(F32)
    white[...] = result.astype(BF16)

    place = pl.ds(row0, tokens)

    def qwen_sends():
        return [
            copy(white, qwen.at[place], mp_sem, (a, o), at(mp=a, dp=rem(dp + o, 8)), (0, o))
            for o in (4, 5, 3, 6, 2, 7, 1, 0) for a in (0, 1) if a == 0 or o
        ]

    def llama_send(c):
        return copy(
            white.at[pl.ds(c * half, half)], llama.at[dp, c], row_sem, (c,),
            at(mp=tp // 8, dp=rem(tp, 8), tp=2 * dp + c), (0,),
        )

    @pl.when(mp == 1)
    def _():
        for c in qwen_sends():
            c.start()
        local = pltpu.make_async_copy(white, qwen.at[place], load_sem.at[3])
        local.start()
        local.wait()

    @pl.when(mp == 0)
    def _():
        llama_send(1).start()

        @pl.when(alone)
        def _():
            local = pltpu.make_async_copy(white.at[pl.ds(0, half)], llama.at[0, 0], load_sem.at[3])
            local.start()
            local.wait()

        @pl.when(jnp.logical_not(alone))
        def _():
            llama_send(0).start()

    @pl.when(jnp.logical_not(alone))
    def _():
        arrived(llama.at[z, core], row_sem, (0,))

    def spread(distance):
        return llama.at[rem(z + distance + 8, 8), core]

    send(spread(0), spread(0), spread_sem, (1,), ahead)
    send(spread(0), spread(0), spread_sem, (5,), behind)
    for step in (1, 2, 3):
        block_a = spread(-sign * step)
        arrived(block_a, spread_sem, (step,))
        send(block_a, block_a, spread_sem, (step + 1,), ahead)
        block_b = spread(sign * step)
        arrived(block_b, spread_sem, (4 + step,))
        if step < 3:
            send(block_b, block_b, spread_sem, (5 + step,), behind)
    arrived(spread(-sign * 4), spread_sem, (4,))
    send(llama.at[:, core], llama.at[:, core], last_sem, (0,), sibling)
    for o in range(1, 8):
        source = pl.multiple_of(rem(dp - o, 8) * tokens, tokens)
        arrived(qwen.at[pl.ds(source, tokens)], mp_sem, (0, o))

    @pl.when(mp == 0)
    def _():
        arrived(qwen.at[place], mp_sem, (0, 0))

    arrived(llama.at[:, 1 - core], last_sem, (0,))
    left = llama[...].reshape(8 * tokens, cols)
    for n in range(cols // TILE):
        here = pl.ds(n * TILE, TILE)
        out[:, here] = lax.dot_general(
            left, qwen[:, here], (((0,), (0,)), ((), ())), preferred_element_type=F32
        ) * (1.0 / math.sqrt(8 * tokens))

    for c in started:
        c.wait_send()

    @pl.when(mp == 1)
    def _():
        for c in qwen_sends():
            c.wait_send()

    @pl.when(mp == 0)
    def _():
        llama_send(1).wait_send()

        @pl.when(jnp.logical_not(alone))
        def _():
            llama_send(0).wait_send()


def body(hidden, down_weight, whitening):
    tokens, units = hidden.shape[1:]
    width, cols = down_weight.shape[2], whitening.shape[2]
    group_rows, side = 2 * tokens, width // 2
    piece = group_rows // 8
    dma = pltpu.SemaphoreType.DMA
    anywhere = pl.BlockSpec(memory_space=pl.ANY)
    return pl.pallas_call(
        kernel,
        out_shape=jax.ShapeDtypeStruct((cols, cols), F32),
        in_specs=[anywhere] * 3,
        out_specs=pl.BlockSpec(memory_space=pltpu.VMEM),
        scratch_shapes=[
            pltpu.VMEM((8 * tokens, units), BF16),
            pltpu.VMEM((units, width), BF16),
            pltpu.VMEM((width, cols), BF16),
            pltpu.VMEM((8, 1, units), F32),
            pltpu.VMEM((4, group_rows, side), F32),
            pltpu.VMEM((4, group_rows, side), F32),
            pltpu.VMEM((4, group_rows, side), F32),
            pltpu.VMEM((4, group_rows, side), BF16),
            pltpu.VMEM((4, 8, piece, side), BF16),
            pltpu.VMEM((8 * tokens, width), BF16),
            pltpu.VMEM((4, group_rows, cols), BF16),
            pltpu.VMEM((tokens, cols), F32),
            pltpu.VMEM((4, 2, tokens, cols), BF16),
            pltpu.VMEM((tokens, cols), BF16),
            pltpu.VMEM((8 * tokens, cols), BF16),
            pltpu.VMEM((8, 2, tokens // 2, cols), BF16),
            dma((4,)),
            dma((2, 14)),
            dma((2, 8)),
            dma((2, 4)),
            dma((2, 4, 8)),
            dma((2, 4, 8)),
            dma((2, 4)),
            dma((2, 4, 2)),
            dma((2, 2, 8)),
            dma((2, 2)),
            dma((2, 8)),
            dma((2, 1)),
        ],
        compiler_params=pltpu.CompilerParams(
            collective_id=0, has_side_effects=True, vmem_limit_bytes=58 * 2**20
        ),
        cost_estimate=pl.CostEstimate(
            flops=5_400_000_000, bytes_accessed=6_000_000, transcendentals=0
        ),
    )(hidden, down_weight, whitening)


def solution(mesh):
    placed = (P("mp", "dp", "tp"), P("mp", "tp", "dp"), P("mp", "dp", "tp"))
    return jax.shard_map(
        body, mesh=mesh, in_specs=placed, out_specs=P(("mp", "dp"), "tp"), check_vma=False
    )
```

```python
import math

import jax
import jax.numpy as jnp
from jax import lax
from jax.experimental import pallas as pl
from jax.experimental.pallas import tpu as pltpu
from jax.sharding import PartitionSpec as P

MESH = pl.DeviceIdType.MESH
F32, BF16 = jnp.float32, jnp.bfloat16
TILE = 256
GROUPS = ((0, 0), (0, 1), (-1, 0), (-1, 1), (1, 0), (1, 1), (2, 0), (2, 1))
DELTAS = (0, -1, 1, 2)
FORWARD = {
    "near": ((10, 2), (0, 3), (5, 8)), "next": ((11, 7), (1, 12), (6, 13)), "far": ((2, 4),), "last": ((7, 9),),
}
PENDING = ((), (), (), (12,), (), (13,), (3, 8), (4, 9))
ORDER = (
    0, 0, "near", 0, "next", 1, 2, 4, 1, 2, 0, "far", 4, 3, 1, 2, 3, "last", 4, 0, 6, 2, 1, 5, 4, 3, 0, 6, 5, 7, 1,
    4, 0, 7, 6, 3, 5, 1, 2, 4, 1, 7, 6, 4, 3, 5, 2, 7, 2, 6, 3, 5, 3, 7, 6, 5, 6, 7, 5, 7,
)


def kernel(
    hid, wgt, fac, out,
    acts, weights, factor, sums, own, give, take, parts, reduced, outs,
    wpart, land, white, rowpart, qwen, llama,
    load_sem, near_sem, sum_sem, pair_sem, ring_sem, all_sem, core_sem, dp_sem, mp_sem, row_sem, spread_sem, last_sem,
):
    mp, tp, dp = lax.axis_index("mp"), lax.axis_index("tp"), lax.axis_index("dp")
    z, core = tp // 2, tp % 2
    y, xlo = dp // 2, dp % 2
    tokens = hid.shape[1]
    half = tokens // 2
    width = wgt.shape[2]
    side = width // 2
    cols = fac.shape[2]

    def at(**coords):
        return {"mp": coords.get("mp", mp), "tp": coords.get("tp", tp), "dp": coords.get("dp", dp)}

    def rem(value, count):
        return lax.rem(value + count, count)

    started = []

    def copy(src, dst, sem, index, target, there=None):
        return pltpu.make_async_remote_copy(
            src_ref=src, dst_ref=dst, send_sem=sem.at[(0, *index)], recv_sem=sem.at[(1, *(there or index))],
            device_id=target, device_id_type=MESH,
        )

    def send(*args, **kw):
        c = copy(*args, **kw)
        c.start()
        started.append(c)

    def arrived(dst, sem, index):
        copy(dst, dst, sem, index, at()).wait_recv()

    row0 = pl.multiple_of(dp * tokens, tokens)
    loads = [
        pltpu.make_async_copy(hid.at[0], acts.at[pl.ds(row0, tokens)], load_sem.at[0]),
        pltpu.make_async_copy(wgt.at[0], weights, load_sem.at[1]),
        pltpu.make_async_copy(fac.at[0], factor, load_sem.at[2]),
    ]
    for load in loads:
        load.start()

    barrier = pltpu.get_barrier_semaphore()
    row_source = mp * 8 + dp
    greet = [at(dp=rem(dp + o, 8)) for o in range(1, 8)]
    greet += [at(tp=rem(tp + 2 * o, 16)) for o in (1, 2, -1, -2)]
    greet += [at(tp=tp + 1 - 2 * core)]
    greet += [at(mp=1 - mp, dp=rem(dp + o, 8)) for o in range(8)]
    for target in greet:
        pl.semaphore_signal(barrier, inc=1, device_id=target, device_id_type=MESH)
    alone = (mp == 0) & (dp == 0) & (tp == 0)

    @pl.when(jnp.logical_not(alone))
    def _():
        pl.semaphore_signal(
            barrier, inc=1, device_id=at(mp=0, dp=z, tp=row_source), device_id_type=MESH
        )

    loads[0].wait()
    sums[dp] = jnp.sum(acts[pl.ds(row0, tokens), :].astype(F32), axis=0, keepdims=True)

    extra = jnp.where(mp == 0, jnp.where(alone, 1, 2), 0)
    pl.semaphore_wait(barrier, len(greet) + extra)

    for o in range(1, 8):
        send(sums.at[dp], sums.at[dp], sum_sem, (o,), at(dp=rem(dp + o, 8)))

    up, down, across = at(dp=rem(dp + 2, 8)), at(dp=rem(dp - 2, 8)), at(dp=dp + 1 - 2 * xlo)

    def rows(dy, other, which):
        x = 1 - xlo if other else xlo
        start = (rem(y + dy + 4, 4) * 2 + x) * tokens + which * half
        return acts.at[pl.ds(pl.multiple_of(start, half), half)]

    hops = {
        0: (up, 0, 0, 0), 1: (up, 0, 0, 1), 2: (up, 0, 1, 0), 3: (up, -1, 0, 0), 4: (up, -1, 1, 0),
        5: (down, 0, 0, 1), 6: (down, 0, 0, 0), 7: (down, 0, 1, 1), 8: (down, 1, 0, 1), 9: (down, 1, 1, 1),
        10: (across, 0, 0, 0), 11: (across, 0, 0, 1), 12: (across, -1, 0, 1), 13: (across, 1, 0, 0),
    }

    def hop(index):
        target, dy, other, which = hops[index]
        block = rows(dy, other, which)
        send(block, block, near_sem, (index,), target)

    def landed(index):
        target, dy, other, which = hops[index]
        if target is up:
            block = rows(dy - 1, other, which)
        elif target is down:
            block = rows(dy + 1, other, which)
        else:
            block = rows(dy, 1 - other, which)
        arrived(block, near_sem, (index,))

    for index in (10, 0, 5, 11, 1, 6):
        hop(index)

    loads[1].wait()
    for o in range(1, 8):
        arrived(sums.at[rem(dp - o, 8)], sum_sem, (o,))
    mean = jnp.sum(sums[...], axis=0) * (1.0 / 1024)
    high = mean.astype(BF16).astype(F32)
    line = lax.broadcasted_iota(jnp.int32, (16, mean.shape[1]), 0)
    pair = jnp.where(line == 0, high, jnp.where(line == 1, mean - high, 0.0)).astype(BF16)
    shift = jnp.sum(jnp.dot(pair, weights[...], preferred_element_type=F32), axis=0, keepdims=True)
    own_shift = jnp.where(core == 0, shift[:, :side], shift[:, side:])
    other_shift = jnp.where(core == 0, shift[:, side:], shift[:, :side])

    sibling = at(tp=tp + 1 - 2 * core)
    sign = 1 - 2 * core

    def along(distance):
        return at(tp=rem(tp + 2 * sign * distance + 16, 16))

    def gather(chunk, sem, index):
        for slot, distance in ((2, 2), (3, -2), (0, 1), (1, -1)):
            send(chunk(0), chunk(0), sem, (*index, slot), along(distance))
        yield
        arrived(chunk(-2), sem, (*index, 2))
        send(chunk(-2), chunk(-2), sem, (*index, 5), along(2))
        send(chunk(-2), chunk(-2), sem, (*index, 4), along(1))
        arrived(chunk(2), sem, (*index, 3))
        send(chunk(2), chunk(2), sem, (*index, 6), along(-1))
        arrived(chunk(-1), sem, (*index, 0))
        arrived(chunk(1), sem, (*index, 1))
        yield
        for slot, distance in ((4, -3), (6, 3), (5, -4)):
            arrived(chunk(distance), sem, (*index, slot))

    def group(g):
        delta, part = GROUPS[g]
        count = tokens if part is not None else 2 * tokens
        piece = count // 8
        base = rem(y + delta + 4, 4) * 2 * tokens
        if part is not None:
            base = base + (1 - xlo if part else xlo) * tokens
        base = pl.multiple_of(base, tokens)
        block = acts.at[pl.ds(base, count)]
        span = pl.ds(0, count)
        for index in PENDING[g]:
            landed(index)

        def partial(dst, first, offset):
            for n in range(side // TILE):
                columns = pl.ds(pl.multiple_of(first + n * TILE, TILE), TILE)
                dst[g, span, pl.ds(n * TILE, TILE)] = (
                    jnp.dot(block[...], weights[:, columns], preferred_element_type=F32)
                    - offset[:, n * TILE:(n + 1) * TILE]
                )

        partial(give, (1 - core) * side, other_shift)
        send(give.at[g, span], take.at[g, span], pair_sem, (g,), sibling)
        partial(own, core * side, own_shift)
        yield
        arrived(take.at[g, span], pair_sem, (g,))
        total = own[g, span, :] + take[g, span, :]
        own[g, span, :] = total
        parts[g, span, :] = total.astype(BF16)

        def rows_for(distance):
            start = rem(z + sign * distance + 8, 8) * piece
            return pl.ds(pl.multiple_of(start, piece), piece)

        def slot_of(slot):
            return reduced.at[g, slot, pl.ds(0, piece)]

        def to_slot(slot, owner, target):
            send(parts.at[g, rows_for(owner)], slot_of(slot), ring_sem, (g, slot), along(target))

        def add(start, slots):
            value = start
            for slot in slots:
                arrived(slot_of(slot), ring_sem, (g, slot))
                value = value + reduced[g, slot, pl.ds(0, piece), :].astype(F32)
            return value

        for slot, owner, target in ((1, 4, 2), (0, 3, 1), (2, -3, -1), (3, 1, 1), (4, -1, -1)):
            to_slot(slot, owner, target)
        yield
        parts[g, rows_for(-2), :] = add(own[g, rows_for(-2), :], (2,)).astype(BF16)
        to_slot(6, -2, -2)
        parts[g, rows_for(2), :] = add(own[g, rows_for(2), :], (0, 1)).astype(BF16)
        to_slot(5, 2, 2)
        yield
        result = add(own[g, rows_for(0), :], (3, 4, 6, 5))
        mine = pl.ds(pl.multiple_of(core * side, side), side)

        def chunk(distance):
            start = base + rem(z + sign * distance + 8, 8) * piece
            return outs.at[pl.ds(pl.multiple_of(start, piece), piece), mine]

        outs[pl.ds(pl.multiple_of(base + z * piece, piece), piece), mine] = result.astype(BF16)
        yield from gather(chunk, all_sem, (g,))
        whole = outs.at[pl.ds(base, count), mine]
        send(whole, whole, core_sem, (g,), sibling)
        yield
        theirs = pl.ds(pl.multiple_of((1 - core) * side, side), side)
        arrived(outs.at[pl.ds(base, count), theirs], core_sem, (g,))
        if g == 0:
            loads[2].wait()
        for n in range(cols // TILE):
            here = pl.ds(n * TILE, TILE)
            wpart[g, span, here] = jnp.dot(
                outs[pl.ds(base, count), :], factor[:, here], preferred_element_type=F32
            ).astype(BF16)
        owner = rem(y + delta + 4, 4) * 2
        d = DELTAS.index(delta)
        for cross in ((0, 1) if part is None else (part,)):
            x = 1 - xlo if cross else xlo
            first = x * tokens if part is None else 0

            def half_to(h, d=d, cross=cross, x=x, first=first):
                slot = jnp.where(mp == 0, h, 2)
                return copy(
                    wpart.at[g, pl.ds(pl.multiple_of(first + h * half, half), half)], land.at[slot, d, cross],
                    dp_sem, (h, d, cross), at(mp=mp * h, dp=owner + x), (slot, d, cross),
                )

            if d or cross:
                for h in (0, 1):
                    c = half_to(h)
                    c.start()
                    started.append(c)
            else:
                first = pl.multiple_of(first, tokens)

                @pl.when(mp == 0)
                def _():
                    for h in (0, 1):
                        land[h, 0, 0] = wpart[g, pl.ds(first + h * half, half), :]

                @pl.when(mp == 1)
                def _():
                    half_to(0).start()
                    land[2, 0, 0] = wpart[g, pl.ds(first + half, half), :]

                late.append(half_to(0))
        yield

    late = []
    groups = [group(g) for g in range(len(GROUPS))]
    for name in ORDER:
        if name in FORWARD:
            for incoming, outgoing in FORWARD[name]:
                landed(incoming)
                hop(outgoing)
        else:
            next(groups[name])

    slots = [(d, cross) for d in range(4) for cross in (0, 1)]

    def llama_send(c):
        return copy(
            rowpart.at[c], llama.at[dp, c], row_sem, (c,), at(mp=tp // 8, dp=rem(tp, 8), tp=2 * dp + c), (0,)
        )

    @pl.when(mp == 0)
    def _():
        for h in (0, 1):
            for d, cross in slots[1:]:
                arrived(land.at[h, d, cross], dp_sem, (h, d, cross))
            value = land[h, 0, 0].astype(F32)
            for d, cross in slots[1:]:
                value = value + land[h, d, cross].astype(F32)
            rowpart[h] = value.astype(BF16)
            if h == 1:
                llama_send(1).start()
            else:

                @pl.when(alone)
                def _():
                    local = pltpu.make_async_copy(rowpart.at[0], llama.at[0, 0], load_sem.at[3])
                    local.start()
                    local.wait()

                @pl.when(jnp.logical_not(alone))
                def _():
                    llama_send(0).start()

        arrived(land.at[2, 0, 0], dp_sem, (2, 0, 0))

    for d, cross in slots[1:]:
        arrived(land.at[2, d, cross], dp_sem, (2, d, cross))
    value = land[2, 0, 0].astype(F32)
    for d, cross in slots[1:]:
        value = value + land[2, d, cross].astype(F32)
    white[...] = value.astype(BF16)

    @pl.when(jnp.logical_not(alone))
    def _():
        arrived(llama.at[z, core], row_sem, (0,))

    def spread(distance):
        return llama.at[rem(z + sign * distance + 8, 8), core]

    def to_sibling(distances):
        for n in distances:
            send(spread(n), spread(n), last_sem, (n + 4,), sibling)

    spreading = gather(spread, spread_sem, ())
    next(spreading)
    for o in (4, 5, 3, 6, 2, 7, 1, 0):
        for other in (1, 0):
            if o or other:
                send(
                    white, qwen.at[dp, mp], mp_sem, (other, o),
                    at(mp=1 - mp if other else mp, dp=rem(dp + o, 8)),
                )
    qwen[dp, mp] = white[...]

    to_sibling((0,))
    next(spreading)
    to_sibling((-2, 2, -1, 1))
    for _ in spreading:
        pass
    to_sibling((-3, 3, -4))
    for other in (0, 1):
        for o in range(8):
            if o or other:
                source = qwen.at[rem(dp - o + 8, 8), 1 - mp if other else mp]
                arrived(source, mp_sem, (other, o))
    for n in (0, -2, 2, -1, 1, -3, 3, -4):
        theirs = llama.at[rem(z - sign * n + 8, 8), 1 - core]
        arrived(theirs, last_sem, (n + 4,))
    left = llama[...].reshape(8 * tokens, cols)
    for n in range(cols // TILE):
        here = pl.ds(n * TILE, TILE)
        out[:, here] = lax.dot_general(
            left, qwen[:, :, :, here].reshape(8 * tokens, TILE), (((0,), (0,)), ((), ())),
            preferred_element_type=F32,
        ) * (1.0 / math.sqrt(8 * tokens))

    for c in started:
        c.wait_send()

    @pl.when(mp == 1)
    def _():
        for c in late:
            c.wait_send()

    @pl.when(mp == 0)
    def _():
        llama_send(1).wait_send()

        @pl.when(jnp.logical_not(alone))
        def _():
            llama_send(0).wait_send()


def body(hidden, down_weight, whitening):
    tokens, units = hidden.shape[1:]
    width, cols = down_weight.shape[2], whitening.shape[2]
    group_rows, side = 2 * tokens, width // 2
    piece, count = group_rows // 8, len(GROUPS)
    dma = pltpu.SemaphoreType.DMA
    anywhere = pl.BlockSpec(memory_space=pl.ANY)
    return pl.pallas_call(
        kernel,
        out_shape=jax.ShapeDtypeStruct((cols, cols), F32),
        in_specs=[anywhere] * 3,
        out_specs=pl.BlockSpec(memory_space=pltpu.VMEM),
        scratch_shapes=[
            pltpu.VMEM((8 * tokens, units), BF16),
            pltpu.VMEM((units, width), BF16),
            pltpu.VMEM((width, cols), BF16),
            pltpu.VMEM((8, 1, units), F32),
            pltpu.VMEM((count, group_rows, side), F32),
            pltpu.VMEM((count, group_rows, side), F32),
            pltpu.VMEM((count, group_rows, side), F32),
            pltpu.VMEM((count, group_rows, side), BF16),
            pltpu.VMEM((count, 7, piece, side), BF16),
            pltpu.VMEM((8 * tokens, width), BF16),
            pltpu.VMEM((count, group_rows, cols), BF16),
            pltpu.VMEM((3, 4, 2, tokens // 2, cols), BF16),
            pltpu.VMEM((tokens // 2, cols), BF16),
            pltpu.VMEM((2, tokens // 2, cols), BF16),
            pltpu.VMEM((8, 2, tokens // 2, cols), BF16),
            pltpu.VMEM((8, 2, tokens // 2, cols), BF16),
            dma((4,)),
            dma((2, 14)),
            dma((2, 8)),
            dma((2, count)),
            dma((2, count, 7)),
            dma((2, count, 7)),
            dma((2, count)),
            dma((2, 3, 4, 2)),
            dma((2, 2, 8)),
            dma((2, 2)),
            dma((2, 7)),
            dma((2, 8)),
        ],
        compiler_params=pltpu.CompilerParams(
            collective_id=0, has_side_effects=True, vmem_limit_bytes=58 * 2**20
        ),
        cost_estimate=pl.CostEstimate(
            flops=5_400_000_000, bytes_accessed=6_000_000, transcendentals=0
        ),
    )(hidden, down_weight, whitening)


def solution(mesh):
    placed = (P("mp", "dp", "tp"), P("mp", "tp", "dp"), P("mp", "dp", "tp"))
    return jax.shard_map(
        body, mesh=mesh, in_specs=placed, out_specs=P(("mp", "dp"), "tp"), check_vma=False
    )
```

```python
import math

import jax
import jax.numpy as jnp
from jax import lax
from jax.experimental import pallas as pl
from jax.experimental.pallas import tpu as pltpu
from jax.sharding import PartitionSpec as P

MESH = pl.DeviceIdType.MESH
F32, BF16 = jnp.float32, jnp.bfloat16
TILE = 256
GROUPS = ((0, 0), (0, 1), (-1, 0), (-1, 1), (1, 0), (1, 1), (2, 0), (2, 1))
DELTAS = (0, -1, 1, 2)
FORWARD = {
    "near": ((10, 2), (0, 3), (5, 8)), "next": ((11, 7), (1, 12), (6, 13)), "far": ((2, 4),), "last": ((7, 9),),
}
PENDING = ((), (), (), (12,), (), (13,), (3, 8), (4, 9))
ORDER = (
    0, 0, "near", 0, "next", 1, 2, 4, 1, 2, 0, "far", 4, 3, 1, 2, 3, "last", 4, 0, 6, 2, 1, 5, 4, 3, 0, 6, 5, 7, 1,
    4, 0, 7, 6, 3, 5, 1, 2, 4, 1, 7, 6, 4, 3, 5, 2, 7, 2, 6, 3, 5, 3, 7, 6, 5, 6, 7, 5, 7,
)


def kernel(
    hid, wgt, fac, out,
    acts, weights, factor, sums, own, give, take, parts, reduced, outs,
    wpart, land, white, rowpart, qwen, llama,
    load_sem, near_sem, sum_sem, pair_sem, ring_sem, all_sem, core_sem, dp_sem, mp_sem, row_sem, spread_sem, last_sem,
):
    mp, tp, dp = lax.axis_index("mp"), lax.axis_index("tp"), lax.axis_index("dp")
    z, core = tp // 2, tp % 2
    y, xlo = dp // 2, dp % 2
    tokens = hid.shape[1]
    half = tokens // 2
    width = wgt.shape[2]
    side = width // 2
    cols = fac.shape[2]

    def at(**coords):
        return {"mp": coords.get("mp", mp), "tp": coords.get("tp", tp), "dp": coords.get("dp", dp)}

    def rem(value, count):
        return lax.rem(value + count, count)

    started = []

    def copy(src, dst, sem, index, target, there=None):
        return pltpu.make_async_remote_copy(
            src_ref=src, dst_ref=dst, send_sem=sem.at[(0, *index)], recv_sem=sem.at[(1, *(there or index))],
            device_id=target, device_id_type=MESH,
        )

    def send(*args, **kw):
        c = copy(*args, **kw)
        c.start()
        started.append(c)

    def arrived(dst, sem, index):
        copy(dst, dst, sem, index, at()).wait_recv()

    row0 = pl.multiple_of(dp * tokens, tokens)
    loads = [
        pltpu.make_async_copy(hid.at[0], acts.at[pl.ds(row0, tokens)], load_sem.at[0]),
        pltpu.make_async_copy(wgt.at[0], weights, load_sem.at[1]),
        pltpu.make_async_copy(fac.at[0], factor, load_sem.at[2]),
    ]
    for load in loads:
        load.start()

    barrier = pltpu.get_barrier_semaphore()
    row_source = mp * 8 + dp
    greet = [at(dp=rem(dp + o, 8)) for o in range(1, 8)]
    greet += [at(tp=rem(tp + 2 * o, 16)) for o in (1, 2, -1, -2)]
    greet += [at(tp=tp + 1 - 2 * core)]
    greet += [at(mp=1 - mp, dp=rem(dp + o, 8)) for o in range(8)]
    for target in greet:
        pl.semaphore_signal(barrier, inc=1, device_id=target, device_id_type=MESH)
    alone = (mp == 0) & (dp == 0) & (tp == 0)

    @pl.when(jnp.logical_not(alone))
    def _():
        pl.semaphore_signal(
            barrier, inc=1, device_id=at(mp=0, dp=z, tp=row_source), device_id_type=MESH
        )

    loads[0].wait()
    sums[dp] = jnp.sum(acts[pl.ds(row0, tokens), :].astype(F32), axis=0, keepdims=True)

    extra = jnp.where(mp == 0, jnp.where(alone, 1, 2), 0)
    pl.semaphore_wait(barrier, len(greet) + extra)

    for o in range(1, 8):
        send(sums.at[dp], sums.at[dp], sum_sem, (o,), at(dp=rem(dp + o, 8)))

    up, down, across = at(dp=rem(dp + 2, 8)), at(dp=rem(dp - 2, 8)), at(dp=dp + 1 - 2 * xlo)

    def rows(dy, other, which):
        x = 1 - xlo if other else xlo
        start = (rem(y + dy + 4, 4) * 2 + x) * tokens + which * half
        return acts.at[pl.ds(pl.multiple_of(start, half), half)]

    hops = {
        0: (up, 0, 0, 0), 1: (up, 0, 0, 1), 2: (up, 0, 1, 0), 3: (up, -1, 0, 0), 4: (up, -1, 1, 0),
        5: (down, 0, 0, 1), 6: (down, 0, 0, 0), 7: (down, 0, 1, 1), 8: (down, 1, 0, 1), 9: (down, 1, 1, 1),
        10: (across, 0, 0, 0), 11: (across, 0, 0, 1), 12: (across, -1, 0, 1), 13: (across, 1, 0, 0),
    }

    def hop(index):
        target, dy, other, which = hops[index]
        block = rows(dy, other, which)
        send(block, block, near_sem, (index,), target)

    def landed(index):
        target, dy, other, which = hops[index]
        if target is up:
            block = rows(dy - 1, other, which)
        elif target is down:
            block = rows(dy + 1, other, which)
        else:
            block = rows(dy, 1 - other, which)
        arrived(block, near_sem, (index,))

    for index in (10, 0, 5, 11, 1, 6):
        hop(index)

    loads[1].wait()
    for o in range(1, 8):
        arrived(sums.at[rem(dp - o, 8)], sum_sem, (o,))
    mean = jnp.sum(sums[...], axis=0) * (1.0 / 1024)
    high = mean.astype(BF16).astype(F32)
    line = lax.broadcasted_iota(jnp.int32, (16, mean.shape[1]), 0)
    pair = jnp.where(line == 0, high, jnp.where(line == 1, mean - high, 0.0)).astype(BF16)
    shift = jnp.sum(jnp.dot(pair, weights[...], preferred_element_type=F32), axis=0, keepdims=True)
    own_shift = jnp.where(core == 0, shift[:, :side], shift[:, side:])
    other_shift = jnp.where(core == 0, shift[:, side:], shift[:, :side])

    sibling = at(tp=tp + 1 - 2 * core)
    sign = 1 - 2 * core

    def along(distance):
        return at(tp=rem(tp + 2 * sign * distance + 16, 16))

    def gather(chunk, sem, index):
        for slot, distance in ((2, 2), (3, -2), (0, 1), (1, -1)):
            send(chunk(0), chunk(0), sem, (*index, slot), along(distance))
        yield
        arrived(chunk(-2), sem, (*index, 2))
        send(chunk(-2), chunk(-2), sem, (*index, 5), along(2))
        send(chunk(-2), chunk(-2), sem, (*index, 4), along(1))
        arrived(chunk(2), sem, (*index, 3))
        send(chunk(2), chunk(2), sem, (*index, 6), along(-1))
        arrived(chunk(-1), sem, (*index, 0))
        arrived(chunk(1), sem, (*index, 1))
        yield
        for slot, distance in ((4, -3), (6, 3), (5, -4)):
            arrived(chunk(distance), sem, (*index, slot))

    def group(g):
        delta, part = GROUPS[g]
        count = tokens if part is not None else 2 * tokens
        piece = count // 8
        base = rem(y + delta + 4, 4) * 2 * tokens
        if part is not None:
            base = base + (1 - xlo if part else xlo) * tokens
        base = pl.multiple_of(base, tokens)
        block = acts.at[pl.ds(base, count)]
        span = pl.ds(0, count)
        for index in PENDING[g]:
            landed(index)

        def partial(dst, first, offset):
            for n in range(side // TILE):
                columns = pl.ds(pl.multiple_of(first + n * TILE, TILE), TILE)
                dst[g, span, pl.ds(n * TILE, TILE)] = (
                    jnp.dot(block[...], weights[:, columns], preferred_element_type=F32)
                    - offset[:, n * TILE:(n + 1) * TILE]
                )

        partial(give, (1 - core) * side, other_shift)
        send(give.at[g, span], take.at[g, span], pair_sem, (g,), sibling)
        partial(own, core * side, own_shift)
        yield
        arrived(take.at[g, span], pair_sem, (g,))
        total = own[g, span, :] + take[g, span, :]
        own[g, span, :] = total
        parts[g, span, :] = total.astype(BF16)

        def rows_for(distance):
            start = rem(z + sign * distance + 8, 8) * piece
            return pl.ds(pl.multiple_of(start, piece), piece)

        def slot_of(slot):
            return reduced.at[g, slot, pl.ds(0, piece)]

        def to_slot(slot, owner, target):
            send(parts.at[g, rows_for(owner)], slot_of(slot), ring_sem, (g, slot), along(target))

        def add(start, slots):
            value = start
            for slot in slots:
                arrived(slot_of(slot), ring_sem, (g, slot))
                value = value + reduced[g, slot, pl.ds(0, piece), :].astype(F32)
            return value

        for slot, owner, target in ((1, 4, 2), (0, 3, 1), (2, -3, -1), (3, 1, 1), (4, -1, -1)):
            to_slot(slot, owner, target)
        yield
        parts[g, rows_for(-2), :] = add(own[g, rows_for(-2), :], (2,)).astype(BF16)
        to_slot(6, -2, -2)
        parts[g, rows_for(2), :] = add(own[g, rows_for(2), :], (0, 1)).astype(BF16)
        to_slot(5, 2, 2)
        yield
        result = add(own[g, rows_for(0), :], (3, 4, 6, 5))
        mine = pl.ds(pl.multiple_of(core * side, side), side)

        def chunk(distance):
            start = base + rem(z + sign * distance + 8, 8) * piece
            return outs.at[pl.ds(pl.multiple_of(start, piece), piece), mine]

        outs[pl.ds(pl.multiple_of(base + z * piece, piece), piece), mine] = result.astype(BF16)
        yield from gather(chunk, all_sem, (g,))
        whole = outs.at[pl.ds(base, count), mine]
        send(whole, whole, core_sem, (g,), sibling)
        yield
        theirs = pl.ds(pl.multiple_of((1 - core) * side, side), side)
        arrived(outs.at[pl.ds(base, count), theirs], core_sem, (g,))
        if g == 0:
            loads[2].wait()
        for n in range(cols // TILE):
            here = pl.ds(n * TILE, TILE)
            wpart[g, span, here] = jnp.dot(
                outs[pl.ds(base, count), :], factor[:, here], preferred_element_type=F32
            ).astype(BF16)
        owner = rem(y + delta + 4, 4) * 2
        d = DELTAS.index(delta)
        for cross in ((0, 1) if part is None else (part,)):
            x = 1 - xlo if cross else xlo
            first = x * tokens if part is None else 0

            def half_to(h, d=d, cross=cross, x=x, first=first):
                slot = jnp.where(mp == 0, h, 2)
                return copy(
                    wpart.at[g, pl.ds(pl.multiple_of(first + h * half, half), half)], land.at[slot, d, cross],
                    dp_sem, (h, d, cross), at(mp=mp * h, dp=owner + x), (slot, d, cross),
                )

            if d or cross:
                for h in (0, 1):
                    c = half_to(h)
                    c.start()
                    started.append(c)
            else:
                first = pl.multiple_of(first, tokens)

                @pl.when(mp == 0)
                def _():
                    for h in (0, 1):
                        land[h, 0, 0] = wpart[g, pl.ds(first + h * half, half), :]

                @pl.when(mp == 1)
                def _():
                    half_to(0).start()
                    land[2, 0, 0] = wpart[g, pl.ds(first + half, half), :]

                late.append(half_to(0))
        yield

    late = []
    groups = [group(g) for g in range(len(GROUPS))]
    for name in ORDER:
        if name in FORWARD:
            for incoming, outgoing in FORWARD[name]:
                landed(incoming)
                hop(outgoing)
        else:
            next(groups[name])

    slots = [(d, cross) for d in range(4) for cross in (0, 1)]

    def llama_send(c):
        return copy(
            rowpart.at[c], llama.at[dp, c], row_sem, (c,), at(mp=tp // 8, dp=rem(tp, 8), tp=2 * dp + c), (0,)
        )

    @pl.when(mp == 0)
    def _():
        for h in (0, 1):
            for d, cross in slots[1:]:
                arrived(land.at[h, d, cross], dp_sem, (h, d, cross))
            value = land[h, 0, 0].astype(F32)
            for d, cross in slots[1:]:
                value = value + land[h, d, cross].astype(F32)
            rowpart[h] = value.astype(BF16)
            if h == 1:
                llama_send(1).start()
            else:

                @pl.when(alone)
                def _():
                    local = pltpu.make_async_copy(rowpart.at[0], llama.at[0, 0], load_sem.at[3])
                    local.start()
                    local.wait()

                @pl.when(jnp.logical_not(alone))
                def _():
                    llama_send(0).start()

        arrived(land.at[2, 0, 0], dp_sem, (2, 0, 0))

    for d, cross in slots[1:]:
        arrived(land.at[2, d, cross], dp_sem, (2, d, cross))
    value = land[2, 0, 0].astype(F32)
    for d, cross in slots[1:]:
        value = value + land[2, d, cross].astype(F32)
    white[...] = value.astype(BF16)

    def qwen_to(offsets):
        for o, other in offsets:
            send(
                white, qwen.at[dp, mp], mp_sem, (other, o),
                at(mp=1 - mp if other else mp, dp=rem(dp + o, 8)),
            )

    qwen_to(((1, 0), (7, 0), (2, 0), (6, 0), (3, 0), (5, 0), (4, 0)))
    @pl.when(jnp.logical_not(alone))
    def _():
        arrived(llama.at[z, core], row_sem, (0,))

    def spread(distance):
        return llama.at[rem(z + sign * distance + 8, 8), core]

    def to_sibling(distances):
        for n in distances:
            send(spread(n), spread(n), last_sem, (n + 4,), sibling)

    spreading = gather(spread, spread_sem, ())
    next(spreading)
    qwen_to(((0, 1), (1, 1), (7, 1), (2, 1), (6, 1), (3, 1), (5, 1), (4, 1)))
    qwen[dp, mp] = white[...]

    to_sibling((0,))
    next(spreading)
    to_sibling((-2, 2, -1, 1))
    for _ in spreading:
        pass
    to_sibling((-3, 3, -4))
    for other in (0, 1):
        for o in range(8):
            if o or other:
                source = qwen.at[rem(dp - o + 8, 8), 1 - mp if other else mp]
                arrived(source, mp_sem, (other, o))
    def half_of(part):
        return llama[:, part].reshape(4 * tokens, cols), qwen[:, part].reshape(4 * tokens, cols)

    def multiply(left, right, n):
        return lax.dot_general(
            left, right[:, n * TILE:(n + 1) * TILE], (((0,), (0,)), ((), ())), preferred_element_type=F32
        )

    left, right = half_of(core)
    for n in range(cols // TILE):
        out[:, pl.ds(n * TILE, TILE)] = multiply(left, right, n)
    for n in (0, -2, 2, -1, 1, -3, 3, -4):
        theirs = llama.at[rem(z - sign * n + 8, 8), 1 - core]
        arrived(theirs, last_sem, (n + 4,))
    left, right = half_of(1 - core)
    for n in range(cols // TILE):
        here = pl.ds(n * TILE, TILE)
        out[:, here] = (out[:, here] + multiply(left, right, n)) * (1.0 / math.sqrt(8 * tokens))

    for c in started:
        c.wait_send()

    @pl.when(mp == 1)
    def _():
        for c in late:
            c.wait_send()

    @pl.when(mp == 0)
    def _():
        llama_send(1).wait_send()

        @pl.when(jnp.logical_not(alone))
        def _():
            llama_send(0).wait_send()


def body(hidden, down_weight, whitening):
    tokens, units = hidden.shape[1:]
    width, cols = down_weight.shape[2], whitening.shape[2]
    group_rows, side = 2 * tokens, width // 2
    piece, count = group_rows // 8, len(GROUPS)
    dma = pltpu.SemaphoreType.DMA
    anywhere = pl.BlockSpec(memory_space=pl.ANY)
    return pl.pallas_call(
        kernel,
        out_shape=jax.ShapeDtypeStruct((cols, cols), F32),
        in_specs=[anywhere] * 3,
        out_specs=pl.BlockSpec(memory_space=pltpu.VMEM),
        scratch_shapes=[
            pltpu.VMEM((8 * tokens, units), BF16),
            pltpu.VMEM((units, width), BF16),
            pltpu.VMEM((width, cols), BF16),
            pltpu.VMEM((8, 1, units), F32),
            pltpu.VMEM((count, group_rows, side), F32),
            pltpu.VMEM((count, group_rows, side), F32),
            pltpu.VMEM((count, group_rows, side), F32),
            pltpu.VMEM((count, group_rows, side), BF16),
            pltpu.VMEM((count, 7, piece, side), BF16),
            pltpu.VMEM((8 * tokens, width), BF16),
            pltpu.VMEM((count, group_rows, cols), BF16),
            pltpu.VMEM((3, 4, 2, tokens // 2, cols), BF16),
            pltpu.VMEM((tokens // 2, cols), BF16),
            pltpu.VMEM((2, tokens // 2, cols), BF16),
            pltpu.VMEM((8, 2, tokens // 2, cols), BF16),
            pltpu.VMEM((8, 2, tokens // 2, cols), BF16),
            dma((4,)),
            dma((2, 14)),
            dma((2, 8)),
            dma((2, count)),
            dma((2, count, 7)),
            dma((2, count, 7)),
            dma((2, count)),
            dma((2, 3, 4, 2)),
            dma((2, 2, 8)),
            dma((2, 2)),
            dma((2, 7)),
            dma((2, 8)),
        ],
        compiler_params=pltpu.CompilerParams(
            collective_id=0, has_side_effects=True, vmem_limit_bytes=58 * 2**20
        ),
        cost_estimate=pl.CostEstimate(
            flops=5_400_000_000, bytes_accessed=6_000_000, transcendentals=0
        ),
    )(hidden, down_weight, whitening)


def solution(mesh):
    placed = (P("mp", "dp", "tp"), P("mp", "tp", "dp"), P("mp", "dp", "tp"))
    return jax.shard_map(
        body, mesh=mesh, in_specs=placed, out_specs=P(("mp", "dp"), "tp"), check_vma=False
    )
```

```python
import math

import jax
import jax.numpy as jnp
from jax import lax
from jax.experimental import pallas as pl
from jax.experimental.pallas import tpu as pltpu
from jax.sharding import PartitionSpec as P

MESH = pl.DeviceIdType.MESH
F32, BF16 = jnp.float32, jnp.bfloat16
TILE = 256
GROUPS = ((0, 0), (0, 1), (-1, 0), (-1, 1), (1, 0), (1, 1), (2, 0), (2, 1))
DELTAS = (0, -1, 1, 2)
FORWARD = {
    "near": ((10, 2), (0, 3), (5, 8)), "next": ((11, 7), (1, 12), (6, 13)), "far": ((2, 4),), "last": ((7, 9),),
}
PENDING = ((), (), (), (12,), (), (13,), (3, 8), (4, 9))
ORDER = (
    0, 0, "near", 0, "next", 1, 2, 4, 1, 2, 0, "far", 4, 3, 1, 2, 3, "last", 4, 0, 6, 2, 1, 5, 4, 3, 0, 6, 5, 7, 1,
    4, 0, 7, 6, 3, 5, 1, 2, 4, 1, 7, 6, 4, 3, 5, 2, 7, 2, 6, 3, 5, 3, 7, 6, 5, 6, 7, 5, 7,
)


def kernel(
    hid, wgt, fac, out,
    acts, weights, factor, sums, own, give, take, parts, reduced, outs,
    wpart, land, white, rowpart, qwen, llama,
    load_sem, near_sem, sum_sem, pair_sem, ring_sem, all_sem, core_sem, dp_sem, mp_sem, row_sem, spread_sem, last_sem,
):
    mp, tp, dp = lax.axis_index("mp"), lax.axis_index("tp"), lax.axis_index("dp")
    z, core = tp // 2, tp % 2
    y, xlo = dp // 2, dp % 2
    tokens = hid.shape[1]
    half = tokens // 2
    width = wgt.shape[2]
    side = width // 2
    cols = fac.shape[2]

    def at(**coords):
        return {"mp": coords.get("mp", mp), "tp": coords.get("tp", tp), "dp": coords.get("dp", dp)}

    def rem(value, count):
        return lax.rem(value + count, count)

    started = []

    def copy(src, dst, sem, index, target, there=None):
        return pltpu.make_async_remote_copy(
            src_ref=src, dst_ref=dst, send_sem=sem.at[(0, *index)], recv_sem=sem.at[(1, *(there or index))],
            device_id=target, device_id_type=MESH,
        )

    def send(*args, **kw):
        c = copy(*args, **kw)
        c.start()
        started.append(c)

    def arrived(dst, sem, index):
        copy(dst, dst, sem, index, at()).wait_recv()

    row0 = pl.multiple_of(dp * tokens, tokens)
    loads = [
        pltpu.make_async_copy(hid.at[0], acts.at[pl.ds(row0, tokens)], load_sem.at[0]),
        pltpu.make_async_copy(wgt.at[0], weights, load_sem.at[1]),
        pltpu.make_async_copy(fac.at[0], factor, load_sem.at[2]),
    ]
    for load in loads:
        load.start()

    barrier = pltpu.get_barrier_semaphore()
    row_source = mp * 8 + dp
    greet = [at(dp=rem(dp + o, 8)) for o in range(1, 8)]
    greet += [at(tp=rem(tp + 2 * o, 16)) for o in (1, 2, -1, -2)]
    greet += [at(tp=tp + 1 - 2 * core)]
    greet += [at(mp=1 - mp, dp=rem(dp + o, 8)) for o in range(8)]
    for target in greet:
        pl.semaphore_signal(barrier, inc=1, device_id=target, device_id_type=MESH)
    alone = (mp == 0) & (dp == 0) & (tp == 0)

    @pl.when(jnp.logical_not(alone))
    def _():
        pl.semaphore_signal(
            barrier, inc=1, device_id=at(mp=0, dp=z, tp=row_source), device_id_type=MESH
        )

    loads[0].wait()
    sums[dp] = jnp.sum(acts[pl.ds(row0, tokens), :].astype(F32), axis=0, keepdims=True)

    extra = jnp.where(mp == 0, jnp.where(alone, 1, 2), 0)
    pl.semaphore_wait(barrier, len(greet) + extra)

    for o in range(1, 8):
        send(sums.at[dp], sums.at[dp], sum_sem, (o,), at(dp=rem(dp + o, 8)))

    up, down, across = at(dp=rem(dp + 2, 8)), at(dp=rem(dp - 2, 8)), at(dp=dp + 1 - 2 * xlo)

    def rows(dy, other, which):
        x = 1 - xlo if other else xlo
        start = (rem(y + dy + 4, 4) * 2 + x) * tokens + which * half
        return acts.at[pl.ds(pl.multiple_of(start, half), half)]

    hops = {
        0: (up, 0, 0, 0), 1: (up, 0, 0, 1), 2: (up, 0, 1, 0), 3: (up, -1, 0, 0), 4: (up, -1, 1, 0),
        5: (down, 0, 0, 1), 6: (down, 0, 0, 0), 7: (down, 0, 1, 1), 8: (down, 1, 0, 1), 9: (down, 1, 1, 1),
        10: (across, 0, 0, 0), 11: (across, 0, 0, 1), 12: (across, -1, 0, 1), 13: (across, 1, 0, 0),
    }

    def hop(index):
        target, dy, other, which = hops[index]
        block = rows(dy, other, which)
        send(block, block, near_sem, (index,), target)

    def landed(index):
        target, dy, other, which = hops[index]
        if target is up:
            block = rows(dy - 1, other, which)
        elif target is down:
            block = rows(dy + 1, other, which)
        else:
            block = rows(dy, 1 - other, which)
        arrived(block, near_sem, (index,))

    for index in (10, 0, 5, 11, 1, 6):
        hop(index)

    loads[1].wait()
    for o in range(1, 8):
        arrived(sums.at[rem(dp - o, 8)], sum_sem, (o,))
    mean = jnp.sum(sums[...], axis=0) * (1.0 / 1024)
    high = mean.astype(BF16).astype(F32)
    line = lax.broadcasted_iota(jnp.int32, (16, mean.shape[1]), 0)
    pair = jnp.where(line == 0, high, jnp.where(line == 1, mean - high, 0.0)).astype(BF16)
    shift = jnp.sum(jnp.dot(pair, weights[...], preferred_element_type=F32), axis=0, keepdims=True)
    own_shift = jnp.where(core == 0, shift[:, :side], shift[:, side:])
    other_shift = jnp.where(core == 0, shift[:, side:], shift[:, :side])

    sibling = at(tp=tp + 1 - 2 * core)
    sign = 1 - 2 * core

    def along(distance):
        return at(tp=rem(tp + 2 * sign * distance + 16, 16))

    def gather(chunk, sem, index):
        for slot, distance in ((2, 2), (3, -2), (0, 1), (1, -1)):
            send(chunk(0), chunk(0), sem, (*index, slot), along(distance))
        yield
        arrived(chunk(-2), sem, (*index, 2))
        send(chunk(-2), chunk(-2), sem, (*index, 5), along(2))
        send(chunk(-2), chunk(-2), sem, (*index, 4), along(1))
        arrived(chunk(2), sem, (*index, 3))
        send(chunk(2), chunk(2), sem, (*index, 6), along(-1))
        arrived(chunk(-1), sem, (*index, 0))
        arrived(chunk(1), sem, (*index, 1))
        yield
        for slot, distance in ((4, -3), (6, 3), (5, -4)):
            arrived(chunk(distance), sem, (*index, slot))

    def group(g):
        delta, part = GROUPS[g]
        count = tokens if part is not None else 2 * tokens
        piece = count // 8
        base = rem(y + delta + 4, 4) * 2 * tokens
        if part is not None:
            base = base + (1 - xlo if part else xlo) * tokens
        base = pl.multiple_of(base, tokens)
        block = acts.at[pl.ds(base, count)]
        span = pl.ds(0, count)
        for index in PENDING[g]:
            landed(index)

        def partial(dst, first, offset):
            for n in range(side // TILE):
                columns = pl.ds(pl.multiple_of(first + n * TILE, TILE), TILE)
                dst[g, span, pl.ds(n * TILE, TILE)] = (
                    jnp.dot(block[...], weights[:, columns], preferred_element_type=F32)
                    - offset[:, n * TILE:(n + 1) * TILE]
                )

        partial(give, (1 - core) * side, other_shift)
        send(give.at[g, span], take.at[g, span], pair_sem, (g,), sibling)
        partial(own, core * side, own_shift)
        yield
        arrived(take.at[g, span], pair_sem, (g,))
        total = own[g, span, :] + take[g, span, :]
        own[g, span, :] = total
        parts[g, span, :] = total.astype(BF16)

        def rows_for(distance):
            start = rem(z + sign * distance + 8, 8) * piece
            return pl.ds(pl.multiple_of(start, piece), piece)

        def slot_of(slot):
            return reduced.at[g, slot, pl.ds(0, piece)]

        def to_slot(slot, owner, target):
            send(parts.at[g, rows_for(owner)], slot_of(slot), ring_sem, (g, slot), along(target))

        def add(start, slots):
            value = start
            for slot in slots:
                arrived(slot_of(slot), ring_sem, (g, slot))
                value = value + reduced[g, slot, pl.ds(0, piece), :].astype(F32)
            return value

        for slot, owner, target in ((1, 4, 2), (0, 3, 1), (2, -3, -1), (3, 1, 1), (4, -1, -1)):
            to_slot(slot, owner, target)
        yield
        parts[g, rows_for(-2), :] = add(own[g, rows_for(-2), :], (2,)).astype(BF16)
        to_slot(6, -2, -2)
        parts[g, rows_for(2), :] = add(own[g, rows_for(2), :], (0, 1)).astype(BF16)
        to_slot(5, 2, 2)
        yield
        result = add(own[g, rows_for(0), :], (3, 4, 6, 5))
        mine = pl.ds(pl.multiple_of(core * side, side), side)

        def chunk(distance):
            start = base + rem(z + sign * distance + 8, 8) * piece
            return outs.at[pl.ds(pl.multiple_of(start, piece), piece), mine]

        outs[pl.ds(pl.multiple_of(base + z * piece, piece), piece), mine] = result.astype(BF16)
        yield from gather(chunk, all_sem, (g,))
        whole = outs.at[pl.ds(base, count), mine]
        send(whole, whole, core_sem, (g,), sibling)
        yield
        theirs = pl.ds(pl.multiple_of((1 - core) * side, side), side)
        arrived(outs.at[pl.ds(base, count), theirs], core_sem, (g,))
        if g == 0:
            loads[2].wait()
        for n in range(cols // TILE):
            here = pl.ds(n * TILE, TILE)
            wpart[g, span, here] = jnp.dot(
                outs[pl.ds(base, count), :], factor[:, here], preferred_element_type=F32
            ).astype(BF16)
        owner = rem(y + delta + 4, 4) * 2
        d = DELTAS.index(delta)
        for cross in ((0, 1) if part is None else (part,)):
            x = 1 - xlo if cross else xlo
            first = x * tokens if part is None else 0

            def half_to(h, d=d, cross=cross, x=x, first=first):
                slot = jnp.where(mp == 0, h, 2)
                return copy(
                    wpart.at[g, pl.ds(pl.multiple_of(first + h * half, half), half)], land.at[slot, d, cross],
                    dp_sem, (h, d, cross), at(mp=mp * h, dp=owner + x), (slot, d, cross),
                )

            if d or cross:
                for h in (0, 1):
                    c = half_to(h)
                    c.start()
                    started.append(c)
            else:
                first = pl.multiple_of(first, tokens)

                @pl.when(mp == 0)
                def _():
                    for h in (0, 1):
                        land[h, 0, 0] = wpart[g, pl.ds(first + h * half, half), :]

                @pl.when(mp == 1)
                def _():
                    half_to(0).start()
                    land[2, 0, 0] = wpart[g, pl.ds(first + half, half), :]

                late.append(half_to(0))
        yield

    late = []
    groups = [group(g) for g in range(len(GROUPS))]
    for name in ORDER:
        if name in FORWARD:
            for incoming, outgoing in FORWARD[name]:
                landed(incoming)
                hop(outgoing)
        else:
            next(groups[name])

    slots = [(d, cross) for d in range(4) for cross in (0, 1)]

    def llama_send(c):
        return copy(
            rowpart.at[c], llama.at[dp, c], row_sem, (c,), at(mp=tp // 8, dp=rem(tp, 8), tp=2 * dp + c), (0,)
        )

    @pl.when(mp == 0)
    def _():
        for h in (0, 1):
            for d, cross in slots[1:]:
                arrived(land.at[h, d, cross], dp_sem, (h, d, cross))
            value = land[h, 0, 0].astype(F32)
            for d, cross in slots[1:]:
                value = value + land[h, d, cross].astype(F32)
            rowpart[h] = value.astype(BF16)
            if h == 1:
                llama_send(1).start()
            else:

                @pl.when(alone)
                def _():
                    local = pltpu.make_async_copy(rowpart.at[0], llama.at[0, 0], load_sem.at[3])
                    local.start()
                    local.wait()

                @pl.when(jnp.logical_not(alone))
                def _():
                    llama_send(0).start()

        arrived(land.at[2, 0, 0], dp_sem, (2, 0, 0))

    for d, cross in slots[1:]:
        arrived(land.at[2, d, cross], dp_sem, (2, d, cross))
    value = land[2, 0, 0].astype(F32)
    for d, cross in slots[1:]:
        value = value + land[2, d, cross].astype(F32)
    white[...] = value.astype(BF16)

    def qwen_to(offsets):
        for o, other in offsets:
            send(
                white, qwen.at[dp, mp], mp_sem, (other, o),
                at(mp=1 - mp if other else mp, dp=rem(dp + o, 8)),
            )

    qwen_to(((1, 0), (7, 0), (2, 0), (6, 0), (3, 0), (5, 0), (4, 0), (0, 1), (1, 1), (7, 1)))
    @pl.when(jnp.logical_not(alone))
    def _():
        arrived(llama.at[z, core], row_sem, (0,))

    def spread(distance):
        return llama.at[rem(z + sign * distance + 8, 8), core]

    def to_sibling(distances):
        for n in distances:
            send(spread(n), spread(n), last_sem, (n + 4,), sibling)

    spreading = gather(spread, spread_sem, ())
    next(spreading)
    qwen_to(((2, 1), (6, 1), (3, 1), (5, 1), (4, 1)))
    qwen[dp, mp] = white[...]

    to_sibling((0,))
    next(spreading)
    to_sibling((-2, 2, -1, 1))
    for _ in spreading:
        pass
    to_sibling((-3, 3, -4))
    for other in (0, 1):
        for o in range(8):
            if o or other:
                source = qwen.at[rem(dp - o + 8, 8), 1 - mp if other else mp]
                arrived(source, mp_sem, (other, o))
    def half_of(part):
        return llama[:, part].reshape(4 * tokens, cols), qwen[:, part].reshape(4 * tokens, cols)

    def multiply(left, right, n):
        return lax.dot_general(
            left, right[:, n * TILE:(n + 1) * TILE], (((0,), (0,)), ((), ())), preferred_element_type=F32
        )

    left, right = half_of(core)
    for n in range(cols // TILE):
        out[:, pl.ds(n * TILE, TILE)] = multiply(left, right, n)
    for n in (0, -2, 2, -1, 1, -3, 3, -4):
        theirs = llama.at[rem(z - sign * n + 8, 8), 1 - core]
        arrived(theirs, last_sem, (n + 4,))
    left, right = half_of(1 - core)
    for n in range(cols // TILE):
        here = pl.ds(n * TILE, TILE)
        out[:, here] = (out[:, here] + multiply(left, right, n)) * (1.0 / math.sqrt(8 * tokens))

    for c in started:
        c.wait_send()

    @pl.when(mp == 1)
    def _():
        for c in late:
            c.wait_send()

    @pl.when(mp == 0)
    def _():
        llama_send(1).wait_send()

        @pl.when(jnp.logical_not(alone))
        def _():
            llama_send(0).wait_send()


def body(hidden, down_weight, whitening):
    tokens, units = hidden.shape[1:]
    width, cols = down_weight.shape[2], whitening.shape[2]
    group_rows, side = 2 * tokens, width // 2
    piece, count = group_rows // 8, len(GROUPS)
    dma = pltpu.SemaphoreType.DMA
    anywhere = pl.BlockSpec(memory_space=pl.ANY)
    return pl.pallas_call(
        kernel,
        out_shape=jax.ShapeDtypeStruct((cols, cols), F32),
        in_specs=[anywhere] * 3,
        out_specs=pl.BlockSpec(memory_space=pltpu.VMEM),
        scratch_shapes=[
            pltpu.VMEM((8 * tokens, units), BF16),
            pltpu.VMEM((units, width), BF16),
            pltpu.VMEM((width, cols), BF16),
            pltpu.VMEM((8, 1, units), F32),
            pltpu.VMEM((count, group_rows, side), F32),
            pltpu.VMEM((count, group_rows, side), F32),
            pltpu.VMEM((count, group_rows, side), F32),
            pltpu.VMEM((count, group_rows, side), BF16),
            pltpu.VMEM((count, 7, piece, side), BF16),
            pltpu.VMEM((8 * tokens, width), BF16),
            pltpu.VMEM((count, group_rows, cols), BF16),
            pltpu.VMEM((3, 4, 2, tokens // 2, cols), BF16),
            pltpu.VMEM((tokens // 2, cols), BF16),
            pltpu.VMEM((2, tokens // 2, cols), BF16),
            pltpu.VMEM((8, 2, tokens // 2, cols), BF16),
            pltpu.VMEM((8, 2, tokens // 2, cols), BF16),
            dma((4,)),
            dma((2, 14)),
            dma((2, 8)),
            dma((2, count)),
            dma((2, count, 7)),
            dma((2, count, 7)),
            dma((2, count)),
            dma((2, 3, 4, 2)),
            dma((2, 2, 8)),
            dma((2, 2)),
            dma((2, 7)),
            dma((2, 8)),
        ],
        compiler_params=pltpu.CompilerParams(
            collective_id=0, has_side_effects=True, vmem_limit_bytes=58 * 2**20
        ),
        cost_estimate=pl.CostEstimate(
            flops=5_400_000_000, bytes_accessed=6_000_000, transcendentals=0
        ),
    )(hidden, down_weight, whitening)


def solution(mesh):
    placed = (P("mp", "dp", "tp"), P("mp", "tp", "dp"), P("mp", "dp", "tp"))
    return jax.shard_map(
        body, mesh=mesh, in_specs=placed, out_specs=P(("mp", "dp"), "tp"), check_vma=False
    )
```

```python
import math

import jax
import jax.numpy as jnp
from jax import lax
from jax.experimental import pallas as pl
from jax.experimental.pallas import tpu as pltpu
from jax.sharding import PartitionSpec as P

MESH = pl.DeviceIdType.MESH
F32, BF16 = jnp.float32, jnp.bfloat16
TILE = 256
GROUPS = ((0, 0), (0, 1), (-1, 0), (-1, 1), (1, 0), (1, 1), (2, 0), (2, 1))
DELTAS = (0, -1, 1, 2)
FORWARD = {
    "near": ((10, 2), (0, 3), (5, 8)), "next": ((11, 7), (1, 12), (6, 13)), "far": ((2, 4),), "last": ((7, 9),),
}
PENDING = ((), (), (), (12,), (), (13,), (3, 8), (4, 9))
ORDER = (
    0, 0, "near", 0, "next", 1, 2, 4, 1, 2, 0, "far", 4, 3, 1, 2, 3, "last", 4, 0, 6, 2, 1, 5, 4, 3, 0, 6, 5, 7, 1,
    4, 0, 7, 6, 3, 5, 1, 2, 4, 1, 7, 6, 4, 3, 5, 2, 7, 2, 6, 3, 5, 3, 7, 6, 5, 6, 7, 5, 7,
)


def kernel(
    hid, wgt, fac, out,
    acts, weights, factor, sums, own, give, take, parts, reduced, outs,
    wpart, land, white, rowpart, qwen, llama,
    load_sem, near_sem, sum_sem, pair_sem, ring_sem, all_sem, core_sem, dp_sem, mp_sem, row_sem, spread_sem, last_sem,
):
    mp, tp, dp = lax.axis_index("mp"), lax.axis_index("tp"), lax.axis_index("dp")
    z, core = tp // 2, tp % 2
    y, xlo = dp // 2, dp % 2
    tokens = hid.shape[1]
    half = tokens // 2
    width = wgt.shape[2]
    side = width // 2
    cols = fac.shape[2]

    def at(**coords):
        return {"mp": coords.get("mp", mp), "tp": coords.get("tp", tp), "dp": coords.get("dp", dp)}

    def rem(value, count):
        return lax.rem(value + count, count)

    started = []

    def copy(src, dst, sem, index, target, there=None):
        return pltpu.make_async_remote_copy(
            src_ref=src, dst_ref=dst, send_sem=sem.at[(0, *index)], recv_sem=sem.at[(1, *(there or index))],
            device_id=target, device_id_type=MESH,
        )

    def send(*args, **kw):
        c = copy(*args, **kw)
        c.start()
        started.append(c)

    def arrived(dst, sem, index):
        copy(dst, dst, sem, index, at()).wait_recv()

    row0 = pl.multiple_of(dp * tokens, tokens)
    loads = [
        pltpu.make_async_copy(hid.at[0], acts.at[pl.ds(row0, tokens)], load_sem.at[0]),
        pltpu.make_async_copy(wgt.at[0], weights, load_sem.at[1]),
        pltpu.make_async_copy(fac.at[0], factor, load_sem.at[2]),
    ]
    for load in loads:
        load.start()

    barrier = pltpu.get_barrier_semaphore()
    row_source = mp * 8 + dp
    greet = [at(dp=rem(dp + o, 8)) for o in range(1, 8)]
    greet += [at(tp=rem(tp + 2 * o, 16)) for o in (1, 2, -1, -2)]
    greet += [at(tp=tp + 1 - 2 * core)]
    greet += [at(mp=1 - mp, dp=rem(dp + o, 8)) for o in range(8)]
    for target in greet:
        pl.semaphore_signal(barrier, inc=1, device_id=target, device_id_type=MESH)
    alone = (mp == 0) & (dp == 0) & (tp == 0)

    @pl.when(jnp.logical_not(alone))
    def _():
        pl.semaphore_signal(
            barrier, inc=1, device_id=at(mp=0, dp=z, tp=row_source), device_id_type=MESH
        )

    loads[0].wait()
    sums[dp] = jnp.sum(acts[pl.ds(row0, tokens), :].astype(F32), axis=0, keepdims=True)

    loads[1].wait()
    for dst, first in ((give, (1 - core) * side), (own, core * side)):
        for n in range(side // TILE):
            columns = pl.ds(pl.multiple_of(first + n * TILE, TILE), TILE)
            dst[0, pl.ds(0, tokens), pl.ds(n * TILE, TILE)] = jnp.dot(
                acts[pl.ds(row0, tokens), :], weights[:, columns], preferred_element_type=F32
            )

    extra = jnp.where(mp == 0, jnp.where(alone, 1, 2), 0)
    pl.semaphore_wait(barrier, len(greet) + extra)

    for o in range(1, 8):
        send(sums.at[dp], sums.at[dp], sum_sem, (o,), at(dp=rem(dp + o, 8)))

    up, down, across = at(dp=rem(dp + 2, 8)), at(dp=rem(dp - 2, 8)), at(dp=dp + 1 - 2 * xlo)

    def rows(dy, other, which):
        x = 1 - xlo if other else xlo
        start = (rem(y + dy + 4, 4) * 2 + x) * tokens + which * half
        return acts.at[pl.ds(pl.multiple_of(start, half), half)]

    hops = {
        0: (up, 0, 0, 0), 1: (up, 0, 0, 1), 2: (up, 0, 1, 0), 3: (up, -1, 0, 0), 4: (up, -1, 1, 0),
        5: (down, 0, 0, 1), 6: (down, 0, 0, 0), 7: (down, 0, 1, 1), 8: (down, 1, 0, 1), 9: (down, 1, 1, 1),
        10: (across, 0, 0, 0), 11: (across, 0, 0, 1), 12: (across, -1, 0, 1), 13: (across, 1, 0, 0),
    }

    def hop(index):
        target, dy, other, which = hops[index]
        block = rows(dy, other, which)
        send(block, block, near_sem, (index,), target)

    def landed(index):
        target, dy, other, which = hops[index]
        if target is up:
            block = rows(dy - 1, other, which)
        elif target is down:
            block = rows(dy + 1, other, which)
        else:
            block = rows(dy, 1 - other, which)
        arrived(block, near_sem, (index,))

    for index in (10, 0, 5, 11, 1, 6):
        hop(index)

    for o in range(1, 8):
        arrived(sums.at[rem(dp - o, 8)], sum_sem, (o,))
    mean = jnp.sum(sums[...], axis=0) * (1.0 / 1024)
    high = mean.astype(BF16).astype(F32)
    line = lax.broadcasted_iota(jnp.int32, (16, mean.shape[1]), 0)
    pair = jnp.where(line == 0, high, jnp.where(line == 1, mean - high, 0.0)).astype(BF16)
    shift = jnp.sum(jnp.dot(pair, weights[...], preferred_element_type=F32), axis=0, keepdims=True)
    own_shift = jnp.where(core == 0, shift[:, :side], shift[:, side:])
    other_shift = jnp.where(core == 0, shift[:, side:], shift[:, :side])

    sibling = at(tp=tp + 1 - 2 * core)
    sign = 1 - 2 * core

    def along(distance):
        return at(tp=rem(tp + 2 * sign * distance + 16, 16))

    def gather(chunk, sem, index):
        for slot, distance in ((2, 2), (3, -2), (0, 1), (1, -1)):
            send(chunk(0), chunk(0), sem, (*index, slot), along(distance))
        yield
        arrived(chunk(-2), sem, (*index, 2))
        send(chunk(-2), chunk(-2), sem, (*index, 5), along(2))
        send(chunk(-2), chunk(-2), sem, (*index, 4), along(1))
        arrived(chunk(2), sem, (*index, 3))
        send(chunk(2), chunk(2), sem, (*index, 6), along(-1))
        arrived(chunk(-1), sem, (*index, 0))
        arrived(chunk(1), sem, (*index, 1))
        yield
        for slot, distance in ((4, -3), (6, 3), (5, -4)):
            arrived(chunk(distance), sem, (*index, slot))

    def group(g):
        delta, part = GROUPS[g]
        count = tokens if part is not None else 2 * tokens
        piece = count // 8
        base = rem(y + delta + 4, 4) * 2 * tokens
        if part is not None:
            base = base + (1 - xlo if part else xlo) * tokens
        base = pl.multiple_of(base, tokens)
        block = acts.at[pl.ds(base, count)]
        span = pl.ds(0, count)
        for index in PENDING[g]:
            landed(index)

        def partial(dst, first, offset):
            if g == 0:
                dst[g, span, :] = dst[g, span, :] - offset
                return
            for n in range(side // TILE):
                columns = pl.ds(pl.multiple_of(first + n * TILE, TILE), TILE)
                dst[g, span, pl.ds(n * TILE, TILE)] = (
                    jnp.dot(block[...], weights[:, columns], preferred_element_type=F32)
                    - offset[:, n * TILE:(n + 1) * TILE]
                )

        partial(give, (1 - core) * side, other_shift)
        send(give.at[g, span], take.at[g, span], pair_sem, (g,), sibling)
        partial(own, core * side, own_shift)
        yield
        arrived(take.at[g, span], pair_sem, (g,))
        total = own[g, span, :] + take[g, span, :]
        own[g, span, :] = total
        parts[g, span, :] = total.astype(BF16)

        def rows_for(distance):
            start = rem(z + sign * distance + 8, 8) * piece
            return pl.ds(pl.multiple_of(start, piece), piece)

        def slot_of(slot):
            return reduced.at[g, slot, pl.ds(0, piece)]

        def to_slot(slot, owner, target):
            send(parts.at[g, rows_for(owner)], slot_of(slot), ring_sem, (g, slot), along(target))

        def add(start, slots):
            value = start
            for slot in slots:
                arrived(slot_of(slot), ring_sem, (g, slot))
                value = value + reduced[g, slot, pl.ds(0, piece), :].astype(F32)
            return value

        for slot, owner, target in ((1, 4, 2), (0, 3, 1), (2, -3, -1), (3, 1, 1), (4, -1, -1)):
            to_slot(slot, owner, target)
        yield
        parts[g, rows_for(-2), :] = add(own[g, rows_for(-2), :], (2,)).astype(BF16)
        to_slot(6, -2, -2)
        parts[g, rows_for(2), :] = add(own[g, rows_for(2), :], (0, 1)).astype(BF16)
        to_slot(5, 2, 2)
        yield
        result = add(own[g, rows_for(0), :], (3, 4, 6, 5))
        mine = pl.ds(pl.multiple_of(core * side, side), side)

        def chunk(distance):
            start = base + rem(z + sign * distance + 8, 8) * piece
            return outs.at[pl.ds(pl.multiple_of(start, piece), piece), mine]

        outs[pl.ds(pl.multiple_of(base + z * piece, piece), piece), mine] = result.astype(BF16)
        yield from gather(chunk, all_sem, (g,))
        whole = outs.at[pl.ds(base, count), mine]
        send(whole, whole, core_sem, (g,), sibling)
        yield
        theirs = pl.ds(pl.multiple_of((1 - core) * side, side), side)
        arrived(outs.at[pl.ds(base, count), theirs], core_sem, (g,))
        if g == 0:
            loads[2].wait()
        for n in range(cols // TILE):
            here = pl.ds(n * TILE, TILE)
            wpart[g, span, here] = jnp.dot(
                outs[pl.ds(base, count), :], factor[:, here], preferred_element_type=F32
            ).astype(BF16)
        owner = rem(y + delta + 4, 4) * 2
        d = DELTAS.index(delta)
        for cross in ((0, 1) if part is None else (part,)):
            x = 1 - xlo if cross else xlo
            first = x * tokens if part is None else 0

            def half_to(h, d=d, cross=cross, x=x, first=first):
                slot = jnp.where(mp == 0, h, 2)
                return copy(
                    wpart.at[g, pl.ds(pl.multiple_of(first + h * half, half), half)], land.at[slot, d, cross],
                    dp_sem, (h, d, cross), at(mp=mp * h, dp=owner + x), (slot, d, cross),
                )

            if d or cross:
                for h in (0, 1):
                    c = half_to(h)
                    c.start()
                    started.append(c)
            else:
                first = pl.multiple_of(first, tokens)

                @pl.when(mp == 0)
                def _():
                    for h in (0, 1):
                        land[h, 0, 0] = wpart[g, pl.ds(first + h * half, half), :]

                @pl.when(mp == 1)
                def _():
                    half_to(0).start()
                    land[2, 0, 0] = wpart[g, pl.ds(first + half, half), :]

                late.append(half_to(0))
        yield

    late = []
    groups = [group(g) for g in range(len(GROUPS))]
    for name in ORDER:
        if name in FORWARD:
            for incoming, outgoing in FORWARD[name]:
                landed(incoming)
                hop(outgoing)
        else:
            next(groups[name])

    slots = [(d, cross) for d in range(4) for cross in (0, 1)]

    def llama_send(c):
        return copy(
            rowpart.at[c], llama.at[dp, c], row_sem, (c,), at(mp=tp // 8, dp=rem(tp, 8), tp=2 * dp + c), (0,)
        )

    @pl.when(mp == 0)
    def _():
        for h in (0, 1):
            for d, cross in slots[1:]:
                arrived(land.at[h, d, cross], dp_sem, (h, d, cross))
            value = land[h, 0, 0].astype(F32)
            for d, cross in slots[1:]:
                value = value + land[h, d, cross].astype(F32)
            rowpart[h] = value.astype(BF16)
            if h == 1:
                llama_send(1).start()
            else:

                @pl.when(alone)
                def _():
                    local = pltpu.make_async_copy(rowpart.at[0], llama.at[0, 0], load_sem.at[3])
                    local.start()
                    local.wait()

                @pl.when(jnp.logical_not(alone))
                def _():
                    llama_send(0).start()

        arrived(land.at[2, 0, 0], dp_sem, (2, 0, 0))

    for d, cross in slots[1:]:
        arrived(land.at[2, d, cross], dp_sem, (2, d, cross))
    value = land[2, 0, 0].astype(F32)
    for d, cross in slots[1:]:
        value = value + land[2, d, cross].astype(F32)
    white[...] = value.astype(BF16)

    def qwen_to(offsets):
        for o, other in offsets:
            send(
                white, qwen.at[dp, mp], mp_sem, (other, o),
                at(mp=1 - mp if other else mp, dp=rem(dp + o, 8)),
            )

    qwen_to(((1, 0), (7, 0), (2, 0), (6, 0), (3, 0), (5, 0), (4, 0), (0, 1), (1, 1), (7, 1)))
    @pl.when(jnp.logical_not(alone))
    def _():
        arrived(llama.at[z, core], row_sem, (0,))

    def spread(distance):
        return llama.at[rem(z + sign * distance + 8, 8), core]

    def to_sibling(distances):
        for n in distances:
            send(spread(n), spread(n), last_sem, (n + 4,), sibling)

    spreading = gather(spread, spread_sem, ())
    next(spreading)
    qwen_to(((2, 1), (6, 1), (3, 1), (5, 1), (4, 1)))
    qwen[dp, mp] = white[...]

    to_sibling((0,))
    next(spreading)
    to_sibling((-2, 2, -1, 1))
    for _ in spreading:
        pass
    to_sibling((-3, 3, -4))
    for other in (0, 1):
        for o in range(8):
            if o or other:
                source = qwen.at[rem(dp - o + 8, 8), 1 - mp if other else mp]
                arrived(source, mp_sem, (other, o))
    def half_of(part):
        return llama[:, part].reshape(4 * tokens, cols), qwen[:, part].reshape(4 * tokens, cols)

    def multiply(left, right, n):
        return lax.dot_general(
            left, right[:, n * TILE:(n + 1) * TILE], (((0,), (0,)), ((), ())), preferred_element_type=F32
        )

    left, right = half_of(core)
    for n in range(cols // TILE):
        out[:, pl.ds(n * TILE, TILE)] = multiply(left, right, n)
    for n in (0, -2, 2, -1, 1, -3, 3, -4):
        theirs = llama.at[rem(z - sign * n + 8, 8), 1 - core]
        arrived(theirs, last_sem, (n + 4,))
    left, right = half_of(1 - core)
    for n in range(cols // TILE):
        here = pl.ds(n * TILE, TILE)
        out[:, here] = (out[:, here] + multiply(left, right, n)) * (1.0 / math.sqrt(8 * tokens))

    for c in started:
        c.wait_send()

    @pl.when(mp == 1)
    def _():
        for c in late:
            c.wait_send()

    @pl.when(mp == 0)
    def _():
        llama_send(1).wait_send()

        @pl.when(jnp.logical_not(alone))
        def _():
            llama_send(0).wait_send()


def body(hidden, down_weight, whitening):
    tokens, units = hidden.shape[1:]
    width, cols = down_weight.shape[2], whitening.shape[2]
    group_rows, side = 2 * tokens, width // 2
    piece, count = group_rows // 8, len(GROUPS)
    dma = pltpu.SemaphoreType.DMA
    anywhere = pl.BlockSpec(memory_space=pl.ANY)
    return pl.pallas_call(
        kernel,
        out_shape=jax.ShapeDtypeStruct((cols, cols), F32),
        in_specs=[anywhere] * 3,
        out_specs=pl.BlockSpec(memory_space=pltpu.VMEM),
        scratch_shapes=[
            pltpu.VMEM((8 * tokens, units), BF16),
            pltpu.VMEM((units, width), BF16),
            pltpu.VMEM((width, cols), BF16),
            pltpu.VMEM((8, 1, units), F32),
            pltpu.VMEM((count, group_rows, side), F32),
            pltpu.VMEM((count, group_rows, side), F32),
            pltpu.VMEM((count, group_rows, side), F32),
            pltpu.VMEM((count, group_rows, side), BF16),
            pltpu.VMEM((count, 7, piece, side), BF16),
            pltpu.VMEM((8 * tokens, width), BF16),
            pltpu.VMEM((count, group_rows, cols), BF16),
            pltpu.VMEM((3, 4, 2, tokens // 2, cols), BF16),
            pltpu.VMEM((tokens // 2, cols), BF16),
            pltpu.VMEM((2, tokens // 2, cols), BF16),
            pltpu.VMEM((8, 2, tokens // 2, cols), BF16),
            pltpu.VMEM((8, 2, tokens // 2, cols), BF16),
            dma((4,)),
            dma((2, 14)),
            dma((2, 8)),
            dma((2, count)),
            dma((2, count, 7)),
            dma((2, count, 7)),
            dma((2, count)),
            dma((2, 3, 4, 2)),
            dma((2, 2, 8)),
            dma((2, 2)),
            dma((2, 7)),
            dma((2, 8)),
        ],
        compiler_params=pltpu.CompilerParams(
            collective_id=0, has_side_effects=True, vmem_limit_bytes=58 * 2**20
        ),
        cost_estimate=pl.CostEstimate(
            flops=5_400_000_000, bytes_accessed=6_000_000, transcendentals=0
        ),
    )(hidden, down_weight, whitening)


def solution(mesh):
    placed = (P("mp", "dp", "tp"), P("mp", "tp", "dp"), P("mp", "dp", "tp"))
    return jax.shard_map(
        body, mesh=mesh, in_specs=placed, out_specs=P(("mp", "dp"), "tp"), check_vma=False
    )
```
